128 devices in a mesh: patch: 32 (over y, z, core), coarse: 4 (over x).
Axes of the slice: x: 4, y: 4, z: 4, core: 2. Of those that a mesh axis runs over, the one named last changes fastest.
Arguments:
- residual: bfloat16 [2, 2, 196608, 256], P(None, None, ('patch', 'coarse')), may hold values from -6 to 6
- patch_inv: bfloat16 [512, 2, 1024, 1024], P(('patch', 'coarse')), may hold values from -0.1875 to 0.1875
- coarse_basis: bfloat16 [512, 2, 1024, 32], P(('patch', 'coarse')), may hold values from -0.1875 to 0.1875
- coarse_inv: bfloat16 [64, 2, 32, 32], P('coarse'), may hold values from -1 to 1
- patch_slots: int32 [512, 512], P(('patch', 'coarse')), may hold values from 0 to 1791, as said below
- send_rows: int32 [128, 2, 128], P(('patch', 'coarse')), may hold values from 0 to 1535, as said below
- coarse_block: int32 [512], P(('patch', 'coarse')), may hold values from 0 to 63
Outputs:
- correction: bfloat16 [2, 2, 196608, 256], P(None, None, ('patch', 'coarse'))
The draws below stay inside these ranges and needn't reach their ends.
Inputs may be any that keep to these rules, and one draw needn't show every extreme that they name: `send_rows`: within each of the two blocks of a device the 128 rows are distinct. `patch_slots`: the 512 positions of a patch are distinct; they hold its device's rows (p mod 4) * 384 to (p mod 4 + 1) * 384 - 1, 64 positions of 1536 or more, and other rows of its device below 1536; each position of 1536 or more is used by exactly one patch of the device.
All inputs are finite; a program needn't handle non-finite values.
Results may differ from the reference program's by a relative error of at most 0.006.
Values may be sent and summed in bfloat16 or wider, within the bound.
A program may use at most 128 MiB of HBM per device.

```python
import jax
import jax.numpy as jnp
from jax import lax

PN = 512
CORE = 384
SLOT = 128
WAVES = 2
CD = 16
PATCH_DEV = 4
RHS = 256
NODE_DEV = 1536
EXT = 1792
REMOTE = 64
PATCHES = 512
NODES = 196608
NBLK = 64


def distinct_order(key, shape):
    length = shape[-1]
    scores = jax.random.randint(key, shape, 0, 1 << 19) * length + jnp.arange(length, dtype=jnp.int32)
    return jnp.argsort(scores, axis=-1, stable=True).astype(jnp.int32)


def draw_send_rows(key, part):
    device_count = PATCHES // PATCH_DEV
    ordering = distinct_order(jax.random.fold_in(key, 5), (device_count, 2, NODE_DEV))
    return ordering[:, :, :SLOT].astype(jnp.int32)


def draw_patch_slots(key, part):
    device_count = PATCHES // PATCH_DEV
    far_count = 2 * SLOT
    far_order = distinct_order(jax.random.fold_in(key, 11), (device_count, far_count))
    remote = NODE_DEV + far_order.reshape(device_count, PATCH_DEV, REMOTE)
    own_count = PN - CORE - REMOTE
    others = NODE_DEV - CORE
    chosen = distinct_order(jax.random.fold_in(key, 13), (device_count, PATCH_DEV, others))[:, :, :own_count]
    patch_index = jnp.arange(PATCH_DEV, dtype=jnp.int32)[None, :, None]
    chosen = jnp.where(chosen >= patch_index * CORE, chosen + CORE, chosen)
    core_rows = jnp.broadcast_to(patch_index * CORE + jnp.arange(CORE, dtype=jnp.int32)[None, None, :], (device_count, PATCH_DEV, CORE))
    listing = jnp.concatenate([core_rows, remote, chosen], axis=-1)
    ordering = distinct_order(jax.random.fold_in(key, 17), (device_count, PATCH_DEV, PN))
    listing = jnp.take_along_axis(listing, ordering, axis=-1)
    return listing.reshape(PATCHES, PN).astype(jnp.int32)


def touch_ends(entries, key, low, largest):
    shape = entries.shape
    index_at = [jax.random.randint(jax.random.fold_in(key, axis), (), 0, shape[axis]) for axis in range(len(shape))]
    entries = entries.at[tuple(index_at)].set(low)
    longest = shape.index(max(shape))
    index_at[longest] = (index_at[longest] + 1) % shape[longest]
    return entries.at[tuple(index_at)].set(largest)


def shard_levels(stream_key, shape, cuts, low, high):
    level = 1.0
    for axis_at, shards_of in cuts:
        steps = jax.random.uniform(jax.random.fold_in(jax.random.fold_in(stream_key, 6), axis_at), (shards_of,), jnp.float32, low / len(cuts), high / len(cuts))
        level = level * jnp.repeat(jnp.exp(steps), shape[axis_at] // shards_of).reshape((-1,) + (1,) * (len(shape) - 1 - axis_at))
    return level


def bell_draw(rng, shape, deviation, bound, split=(), held_as=jnp.bfloat16):
    level = shard_levels(rng, shape, split, -0.22, 0.18) if split else 1.0
    drawn = jax.random.normal(rng, shape, jnp.float32) * deviation * level
    return jnp.minimum(jnp.maximum(drawn, -bound), bound).astype(held_as)


def setup_inputs(seed: int = 0) -> dict:
    keys = jax.random.split(jax.random.key(seed), 8)
    residual = bell_draw(keys[0], (WAVES, 2, NODES, RHS), 1.0, 6.0, ((2, 128),))
    patch_inv = bell_draw(keys[1], (PATCHES, WAVES, 2 * PN, 2 * PN), (2 * PN) ** -0.5, 0.1875, ((0, 128),))
    coarse_basis = bell_draw(keys[2], (PATCHES, WAVES, 2 * PN, 2 * CD), (2 * PN) ** -0.5, 0.1875, ((0, 128),))
    coarse_inv = bell_draw(keys[3], (NBLK, WAVES, 2 * CD, 2 * CD), (2 * CD) ** -0.5, 1.0, ((0, 4),))
    patch_slots = draw_patch_slots(jax.random.fold_in(keys[7], 71), 0)
    send_rows = draw_send_rows(jax.random.fold_in(keys[7], 71), 0)
    coarse_block = touch_ends(jax.random.randint(keys[6], (PATCHES,), 0, NBLK), jax.random.fold_in(keys[6], 1), 0, NBLK - 1).astype(jnp.int32)
    return {"residual": residual, "patch_inv": patch_inv, "coarse_basis": coarse_basis, "coarse_inv": coarse_inv, "patch_slots": patch_slots, "send_rows": send_rows, "coarse_block": coarse_block}


def reference(residual, patch_inv, coarse_basis, coarse_inv, patch_slots, send_rows, coarse_block):
    device_count = PATCHES // PATCH_DEV
    node_data = residual.reshape(WAVES, 2, device_count, NODE_DEV, RHS)
    device_ids = jnp.arange(device_count, dtype=jnp.int32)
    highest = lax.Precision.HIGHEST

    def gather_patches(device):
        below = (device - 1) % device_count
        above = (device + 1) % device_count
        own_rows = node_data[:, :, device]
        from_below = jnp.take(node_data[:, :, below], send_rows[below, 0], axis=2)
        from_above = jnp.take(node_data[:, :, above], send_rows[above, 1], axis=2)
        extended = jnp.concatenate([own_rows, from_below, from_above], axis=2)
        slot_list = lax.dynamic_slice_in_dim(patch_slots, device * PATCH_DEV, PATCH_DEV, 0)
        return jnp.take(extended, slot_list, axis=2), slot_list

    def basis_of(device):
        basis_rows = lax.dynamic_slice_in_dim(coarse_basis, device * PATCH_DEV, PATCH_DEV, 0)
        return basis_rows.astype(jnp.float32).reshape(PATCH_DEV, WAVES, 2, PN, 2 * CD)

    def restrict(device):
        gathered, slot_list = gather_patches(device)
        return jnp.einsum('pwqnc,wqpnr->pwcr', basis_of(device), gathered.astype(jnp.float32), precision=highest)

    patch_parts = lax.map(restrict, device_ids).reshape(PATCHES, WAVES, 2 * CD, RHS)
    coarse_sums = jax.ops.segment_sum(patch_parts, coarse_block, NBLK)
    coarse_coef = jnp.einsum('bwcd,bwdr->bwcr', coarse_inv.astype(jnp.float32), coarse_sums, precision=highest).astype(jnp.bfloat16)

    def correct(device):
        gathered, slot_list = gather_patches(device)
        inverse = lax.dynamic_slice_in_dim(patch_inv, device * PATCH_DEV, PATCH_DEV, 0)
        inverse = inverse.astype(jnp.float32).reshape(PATCH_DEV, WAVES, 2, PN, 2, PN)
        local_terms = jnp.einsum('pwabqn,wqpnr->wapbr', inverse, gathered.astype(jnp.float32), precision=highest)
        block_ids = lax.dynamic_slice_in_dim(coarse_block, device * PATCH_DEV, PATCH_DEV, 0)
        patch_coef = jnp.take(coarse_coef, block_ids, axis=0).astype(jnp.float32)
        local_terms = local_terms + jnp.einsum('pwqnc,pwcr->wqpnr', basis_of(device), patch_coef, precision=highest)
        collected = jnp.zeros((WAVES, 2, EXT, RHS), jnp.float32).at[:, :, slot_list].add(local_terms)
        return collected[:, :, :NODE_DEV], collected[:, :, NODE_DEV:NODE_DEV + SLOT], collected[:, :, NODE_DEV + SLOT:]

    own_terms, to_lower, to_upper = lax.map(correct, device_ids)

    def finish(device):
        below = (device - 1) % device_count
        above = (device + 1) % device_count
        summed = own_terms[device]
        summed = summed.at[:, :, send_rows[device, 0]].add(to_lower[above])
        summed = summed.at[:, :, send_rows[device, 1]].add(to_upper[below])
        return summed.astype(jnp.bfloat16)

    finished = lax.map(finish, device_ids)
    return jnp.moveaxis(finished, 0, 2).reshape(WAVES, 2, NODES, RHS)
```

```python
import functools

import jax
import jax.numpy as jnp
from jax import lax
from jax.experimental import pallas as pl
from jax.experimental.pallas import tpu as pltpu
from jax.sharding import PartitionSpec as P

MESH = pl.DeviceIdType.MESH
F32 = jnp.float32
BF16 = jnp.bfloat16
NODE = 1536
CORE = 384
PN = 512
XS = 4
GM = 8
HALF = 1024


def dot(a, b):
    return lax.dot_general(a, b, (((1,), (0,)), ((), ())), preferred_element_type=F32)


def dot_t(a, b):
    return lax.dot_general(a, b, (((1,), (1,)), ((), ())), preferred_element_type=F32)


def iota(shape, axis):
    return lax.broadcasted_iota(jnp.int32, shape, axis).astype(F32)


def hot(mask):
    return jnp.where(mask, 1.0, 0.0).astype(BF16)


def columns(row):
    return jnp.transpose(jnp.broadcast_to(row, (128, 128)))


def kernel(
    groups,
    res_hbm, inv_hbm, basis_hbm, cinv_hbm, slots_ref, send_ref, cb_ref,
    out_ref,
    res_v, inv_v, basis_v, cinv_v, ci_v,
    krow_s, ss, sst, sel_o, sel_ot, sel_r, sel_rt, perm, permt,
    hs1, hr1, hs2, hr2, u, gath, bt, bp, cbig, own, yor, yo, yr,
    cbt, cbr, oh, oht, sb1, xb, db, s2, cgs, cg, rb, cf,
    load_sem, inv_sem, hs_sem, hr_sem, hs2_sem, hr2_sem,
    cb_ss, cb_rs, ci_ss, ci_rs, a_ss, a_rs, b_ss, b_rs, c_ss, c_rs, d_ss, d_rs,
):
    pidx = lax.axis_index("patch")
    x = lax.axis_index("coarse")
    g = pidx // 2
    h = pidx % 2
    m = h * XS + x
    me = pidx * XS + x
    count = groups * GM
    per_owner = 32 // groups
    orow = per_owner * 32

    def at_member(mm):
        return (g * 2 + mm // XS, mm % XS)

    def at_group(gg):
        return (gg * 2 + h, x)

    def at_device(d):
        return (d // XS, d % XS)

    upper = at_device((me + 1) % count)
    lower = at_device((me + count - 1) % count)

    def remote(src, dst, ssem, rsem, dev):
        return pltpu.make_async_remote_copy(
            src_ref=src, dst_ref=dst, send_sem=ssem, recv_sem=rsem,
            device_id=dev, device_id_type=MESH,
        )

    loads = [
        pltpu.make_async_copy(res_hbm.at[i // 2, i % 2], res_v.at[i], load_sem.at[i])
        for i in range(4)
    ]
    loads.append(pltpu.make_async_copy(basis_hbm, basis_v, load_sem.at[4]))
    loads.append(pltpu.make_async_copy(cinv_hbm, cinv_v, load_sem.at[5]))
    for copy in loads:
        copy.start()

    def inv_copy(i):
        return pltpu.make_async_copy(inv_hbm.at[i // 2, i % 2], inv_v.at[i], inv_sem.at[i])

    for i in range(8):
        inv_copy(i).start()

    barrier = pltpu.get_barrier_semaphore()
    peers = [upper, lower]
    peers += [at_member((m + k) % GM) for k in range(1, GM)]
    peers += [at_group((g + k) % groups) for k in range(1, groups)]
    for dev in peers:
        pl.semaphore_signal(barrier, inc=1, device_id=dev, device_id_type=MESH)

    for b in range(2):
        row = send_ref[0, b : b + 1, :].astype(F32)
        col = columns(row)
        for t in range(NODE // 128):
            ss[128 * b : 128 * b + 128, 128 * t : 128 * t + 128] = hot(
                col == iota((128, 128), 1) + float(128 * t)
            )
        sst[:, 128 * b : 128 * b + 128] = hot(iota((NODE, 128), 0) == row)

    lane = lax.broadcasted_iota(jnp.int32, (8, 128), 1)
    target = jnp.where(
        lane < 64,
        jnp.where(lane < 32, cb_ref[0], cb_ref[1]),
        jnp.where(lane < 96, cb_ref[2], cb_ref[3]),
    ) * 32 + lane % 32
    cbt[...] = target.astype(F32)
    cbr[0] = target.astype(F32)

    def halo_out(w4, b):
        return remote(
            hs1.at[w4, pl.ds(128 * b, 128)], hr1.at[w4, pl.ds(128 * b, 128)],
            hs_sem.at[w4, b], hr_sem.at[w4, b], upper if b == 0 else lower,
        )

    for w4 in range(4):
        loads[w4].wait()
        hs1[w4] = dot(ss[...], res_v[w4]).astype(BF16)
        if w4 == 0:
            pl.semaphore_wait(barrier, len(peers))
        for b in range(2):
            halo_out(w4, b).start()

    def cb_out(k):
        return remote(cbt, cbr.at[k], cb_ss.at[k], cb_rs.at[k], at_member((m + k) % GM))

    for k in range(1, GM):
        cb_out(k).start()
    loads[5].wait()
    first = 32 * h + per_owner * g
    holder = first // 16
    mine = cinv_v.at[pl.ds(first % 16, per_owner)]

    def ci_out(k):
        return remote(mine, ci_v, ci_ss.at[k], ci_rs, (pidx, (x + k) % XS))

    @pl.when(x == holder)
    def _():
        for k in range(1, XS):
            ci_out(k).start()
        ci_v[...] = cinv_v[pl.ds(first % 16, per_owner)]

    s = slots_ref[...].astype(F32)
    base = iota((4, PN), 0) * float(CORE)
    is_rem = s >= float(NODE)
    is_core = (s >= base) & (s < base + float(CORE))
    weight = jnp.where(is_rem, 256.0, jnp.where(is_core, 0.0, 1.0)).astype(BF16)
    tri = hot(iota((PN, PN), 0) < iota((PN, PN), 1))
    ranks = dot(weight, tri)
    rank_r = jnp.floor(ranks * (1.0 / 256.0))
    rank_o = ranks - 256.0 * rank_r
    place = jnp.where(is_core, s - base, jnp.where(is_rem, 448.0 + rank_r, 384.0 + rank_o))
    for p in range(4):
        krow_s[p] = place[p : p + 1, :]

    def build(p, carry):
        krow = krow_s[p]
        permt[p] = hot(iota((PN, PN), 0) == krow)
        for c in range(4):
            col = columns(krow[:, 128 * c : 128 * c + 128])
            for t in range(4):
                perm[p, 128 * c : 128 * c + 128, 128 * t : 128 * t + 128] = hot(
                    col == iota((128, 128), 1) + float(128 * t)
                )
        return carry

    lax.fori_loop(0, 4, build, 0)
    s_hi = jnp.floor(s * (1.0 / 128.0))
    s_lo = s - 128.0 * s_hi
    s_hi, s_lo = s_hi.astype(BF16), s_lo.astype(BF16)
    values = []
    for p in range(4):
        tail = perm[p, :, 384:512]
        values.append((128.0 * dot(s_hi, tail) + dot(s_lo, tail))[p : p + 1, :])
    low_lane = lax.broadcasted_iota(jnp.int32, (1, 128), 1) < 64
    for j in range(2):
        v0, v1 = values[2 * j], values[2 * j + 1]
        row_o = jnp.where(low_lane, v0, pltpu.roll(v1, 64, 1))
        row_r = jnp.where(low_lane, pltpu.roll(v0, 64, 1), v1) - float(NODE)
        here = slice(128 * j, 128 * j + 128)
        col = columns(row_o)
        for t in range(NODE // 128):
            sel_o[here, 128 * t : 128 * t + 128] = hot(
                col == iota((128, 128), 1) + float(128 * t)
            )
        sel_ot[:, here] = hot(iota((NODE, 128), 0) == row_o)
        col = columns(row_r)
        for t in range(2):
            sel_r[here, 128 * t : 128 * t + 128] = hot(
                col == iota((128, 128), 1) + float(128 * t)
            )
        sel_rt[:, here] = hot(iota((256, 128), 0) == row_r)

    for w4 in range(4):
        others = dot(sel_o[...], res_v[w4]).astype(BF16)
        for p in range(4):
            u[p, w4, 0:CORE] = res_v[w4, CORE * p : CORE * p + CORE]
            u[p, w4, CORE : CORE + 64] = others[64 * p : 64 * p + 64]

    loads[4].wait()
    eye = hot(iota((32, 32), 0) == iota((32, 32), 1))

    def bases(p, carry):
        for w in range(2):
            bt[p, w] = dot_t(eye, basis_v[p, w]).astype(BF16)
            for q in range(2):
                i = 2 * w + q
                bp[p, :, 32 * i : 32 * i + 32] = dot(
                    permt[p], basis_v[p, w, PN * q : PN * q + PN]
                ).astype(BF16)
        return carry

    lax.fori_loop(0, 4, bases, 0)
    cbig[...] = jnp.zeros_like(cbig)

    offset = (h * HALF).astype(F32)
    for k in range(GM):
        if k:
            cb_out(k).wait_recv()
        row = cbr[k, 0:1, :] - offset
        here = slice(128 * k, 128 * k + 128)
        oht[:, here] = hot(iota((HALF, 128), 0) == row)
        col = columns(row)
        for t in range(HALF // 128):
            oh[here, 128 * t : 128 * t + 128] = hot(col == iota((128, 128), 1) + float(128 * t))

    for w4 in range(4):
        for b in range(2):
            halo_out(w4, b).wait_recv()
        far = dot(sel_r[...], hr1[w4]).astype(BF16)
        for p in range(4):
            u[p, w4, CORE + 64 : PN] = far[64 * p : 64 * p + 64]

    def gather(p, carry):
        for w in range(2):
            for q in range(2):
                gath[p, w, PN * q : PN * q + PN] = dot(perm[p], u[p, 2 * w + q]).astype(BF16)
            part = dot(bt[p, w], gath[p, w]).astype(BF16)
            for e in range(2):
                sb1[2 * w + e, pl.ds(32 * p, 32)] = part[:, 128 * e : 128 * e + 128]
        return carry

    lax.fori_loop(0, 4, gather, 0)

    def stage_a(k):
        mm = (m + k) % GM
        return remote(sb1.at[mm % XS], xb.at[pl.ds(128 * k, 128)], a_ss.at[k], a_rs.at[k], at_member(mm))

    for k in range(1, GM):
        stage_a(k).start()
    xb[0:128] = sb1[x]

    def local(i, carry):
        p, w = i // 2, i % 2
        inv_copy(i).wait()
        for q in range(2):
            loc = dot(inv_v[i, PN * q : PN * q + PN, :], gath[p, w]).astype(BF16)
            y = dot(permt[p], loc)
            own[2 * w + q, pl.ds(pl.multiple_of(CORE * p, CORE), CORE)] = y[0:CORE]
            yor[2 * w + q, p] = y[CORE:PN]
        return carry

    lax.fori_loop(0, 3, local, 0)

    for k in range(1, GM):
        stage_a(k).wait_recv()
    db[...] = dot(oht[...], xb[...]).astype(BF16)

    def stage_b(k):
        gg = (g + k) % groups
        return remote(
            db.at[pl.ds(pl.multiple_of(orow * gg, orow), orow)], s2.at[k],
            b_ss.at[k], b_rs.at[k], at_group(gg),
        )

    for k in range(1, groups):
        stage_b(k).start()

    lax.fori_loop(3, 6, local, 0)

    own_rows = pl.ds(pl.multiple_of(orow * g, orow), orow)
    total = db[own_rows].astype(F32)
    for k in range(1, groups):
        stage_b(k).wait_recv()
        total = total + s2[k].astype(F32)
    t_hi = total.astype(BF16)
    t_lo = (total - t_hi.astype(F32)).astype(BF16)

    @pl.when(x != holder)
    def _():
        ci_out(1).wait_recv()

    for b in range(per_owner):
        inv_b = ci_v[b, x // 2]
        rows = slice(32 * b, 32 * b + 32)
        cgs[rows] = (dot(inv_b, t_hi[rows]) + dot(inv_b, t_lo[rows])).astype(BF16)

    def stage_c(k):
        return remote(cgs, cg.at[own_rows], c_ss.at[k], c_rs.at[k], at_group((g + k) % groups))

    for k in range(1, groups):
        stage_c(k).start()
    cg[own_rows] = cgs[...]

    lax.fori_loop(6, 8, local, 0)

    for k in range(1, groups):
        stage_c(k).wait_recv()
    rb[...] = dot(oh[...], cg[...]).astype(BF16)

    def stage_d(k):
        return remote(
            rb.at[pl.ds(128 * k, 128)], cf.at[h, x], d_ss.at[k], d_rs.at[k],
            at_member((m + GM - k) % GM),
        )

    for k in range(1, GM):
        stage_d(k).start()
    cf[h, x] = rb[0:128]
    for k in range(1, GM):
        stage_d(k).wait_recv()

    for w in range(2):
        for e in range(2):
            both = cf[0, 2 * w + e] + cf[1, 2 * w + e]
            for p in range(4):
                for q in range(2):
                    i = 2 * w + q
                    cbig[p, 32 * i : 32 * i + 32, 256 * i + 128 * e : 256 * i + 128 * e + 128] = both[
                        32 * p : 32 * p + 32
                    ]
    for p in range(4):
        part = dot(bp[p, 448:512], cbig[p])
        for w4 in range(4):
            yr[w4, 64 * p : 64 * p + 64] = (
                yor[w4, p, 64:128] + part[:, 256 * w4 : 256 * w4 + 256]
            ).astype(BF16)

    def back(w4, b):
        return remote(
            hs2.at[w4, pl.ds(128 * b, 128)], hr2.at[w4, pl.ds(128 * b, 128)],
            hs2_sem.at[w4, b], hr2_sem.at[w4, b], lower if b == 0 else upper,
        )

    for w4 in range(4):
        hs2[w4] = dot(sel_rt[...], yr[w4]).astype(BF16)
        for b in range(2):
            back(w4, b).start()

    def coarse_own(p, carry):
        rows = pl.ds(pl.multiple_of(CORE * p, CORE), CORE)
        for w4 in range(4):
            part = dot(bp[p, 0:448], cbig[p, :, 256 * w4 : 256 * w4 + 256])
            own[w4, rows] += part[0:CORE]
            yo[w4, pl.ds(pl.multiple_of(64 * p, 64), 64)] = (
                yor[w4, p, 0:64] + part[CORE:448]
            ).astype(BF16)
        return carry

    lax.fori_loop(0, 4, coarse_own, 0)

    def spread(w4, carry):
        own[w4] += dot(sel_ot[...], yo[w4])
        return carry

    lax.fori_loop(0, 4, spread, 0)

    for w4 in range(4):
        for b in range(2):
            back(w4, b).wait_recv()
        out_ref[w4 // 2, w4 % 2] = (own[w4] + dot(sst[...], hr2[w4])).astype(BF16)

    for w4 in range(4):
        for b in range(2):
            halo_out(w4, b).wait_send()
            back(w4, b).wait_send()
    for k in range(1, GM):
        cb_out(k).wait_send()
        stage_a(k).wait_send()
        stage_d(k).wait_send()
    for k in range(1, groups):
        stage_b(k).wait_send()
        stage_c(k).wait_send()

    @pl.when(x == holder)
    def _():
        for k in range(1, XS):
            ci_out(k).wait_send()


def solution(mesh):
    groups = mesh.shape["patch"] // 2
    per_owner = 32 // groups
    vm = pltpu.VMEM
    dma = pltpu.SemaphoreType.DMA
    scratch = [
        vm((4, NODE, 256), BF16), vm((8, 1024, 1024), BF16), vm((4, 2, 1024, 32), BF16),
        vm((16, 2, 32, 32), BF16), vm((per_owner, 2, 32, 32), BF16),
        vm((4, 1, PN), F32),
        vm((256, NODE), BF16), vm((NODE, 256), BF16),
        vm((256, NODE), BF16), vm((NODE, 256), BF16),
        vm((256, 256), BF16), vm((256, 256), BF16),
        vm((4, PN, PN), BF16), vm((4, PN, PN), BF16),
        vm((4, 256, 256), BF16), vm((4, 256, 256), BF16),
        vm((4, 256, 256), BF16), vm((4, 256, 256), BF16),
        vm((4, 4, PN, 256), BF16), vm((4, 2, 1024, 256), BF16),
        vm((4, 2, 32, 1024), BF16), vm((4, PN, 128), BF16), vm((4, 128, 1024), BF16),
        vm((4, NODE, 256), F32), vm((4, 4, 128, 256), F32),
        vm((4, 256, 256), BF16), vm((4, 256, 256), BF16),
        vm((8, 128), F32), vm((GM, 8, 128), F32),
        vm((HALF, HALF), BF16), vm((HALF, HALF), BF16),
        vm((4, 128, 128), BF16), vm((HALF, 128), BF16), vm((HALF, 128), BF16),
        vm((groups, 32 * per_owner, 128), BF16), vm((32 * per_owner, 128), BF16),
        vm((HALF, 128), BF16), vm((HALF, 128), BF16), vm((2, 4, 128, 128), BF16),
        dma((6,)), dma((8,)), dma((4, 2)), dma((4, 2)), dma((4, 2)), dma((4, 2)),
        dma((GM,)), dma((GM,)), dma((XS,)), dma,
        dma((GM,)), dma((GM,)), dma((groups,)), dma((groups,)),
        dma((groups,)), dma((groups,)), dma((GM,)), dma((GM,)),
    ]

    def per_device(residual, patch_inv, coarse_basis, coarse_inv, patch_slots, send_rows, coarse_block):
        hbm = pl.BlockSpec(memory_space=pl.ANY)
        vmem = pl.BlockSpec(memory_space=pltpu.VMEM)
        return pl.pallas_call(
            functools.partial(kernel, groups),
            out_shape=jax.ShapeDtypeStruct(residual.shape, BF16),
            in_specs=[hbm, hbm, hbm, hbm, vmem, vmem, pl.BlockSpec(memory_space=pltpu.SMEM)],
            out_specs=vmem,
            scratch_shapes=scratch,
            compiler_params=pltpu.CompilerParams(
                collective_id=0, has_side_effects=True, vmem_limit_bytes=62 * 1024 * 1024
            ),
        )(residual, patch_inv, coarse_basis, coarse_inv, patch_slots, send_rows, coarse_block)

    node = P(None, None, ("patch", "coarse"), None)
    both = ("patch", "coarse")
    return jax.shard_map(
        per_device,
        mesh=mesh,
        in_specs=(
            node, P(both, None, None, None), P(both, None, None, None),
            P("coarse", None, None, None), P(both, None), P(both, None, None), P(both),
        ),
        out_specs=node,
        check_vma=False,
    )
```

```python
import functools

import jax
import jax.numpy as jnp
from jax import lax
from jax.experimental import pallas as pl
from jax.experimental.pallas import tpu as pltpu
from jax.sharding import PartitionSpec as P

MESH = pl.DeviceIdType.MESH
F32 = jnp.float32
BF16 = jnp.bfloat16
NODE = 1536
CORE = 384
PN = 512
XS = 4
GM = 8
HALF = 1024


def dot(a, b):
    return lax.dot_general(a, b, (((1,), (0,)), ((), ())), preferred_element_type=F32)


def dot_t(a, b):
    return lax.dot_general(a, b, (((1,), (1,)), ((), ())), preferred_element_type=F32)


def iota(shape, axis):
    return lax.broadcasted_iota(jnp.int32, shape, axis).astype(F32)


def hot(mask):
    return jnp.where(mask, 1.0, 0.0).astype(BF16)


def columns(row):
    return jnp.transpose(jnp.broadcast_to(row, (128, 128)))


def kernel(
    groups,
    res_hbm, inv_hbm, basis_hbm, cinv_hbm, slots_ref, send_ref, cb_ref,
    out_ref,
    res_v, inv_v, basis_v, cinv_v, ci_v,
    krow_s, ss, sst, sel_o, sel_ot, sel_r, sel_rt, perm, permt,
    hs1, hr1, hs2, hr2, u, gath, bp, cbig, own, yor, yo, yr,
    cbt, cbr, oh, oht, sb1, xb, db, s2, cgs, cg, rb, cf,
    load_sem, inv_sem, hs_sem, hr_sem, hs2_sem, hr2_sem,
    cb_ss, cb_rs, ci_ss, ci_rs, a_ss, a_rs, b_ss, b_rs, c_ss, c_rs, d_ss, d_rs,
):
    pidx = lax.axis_index("patch")
    x = lax.axis_index("coarse")
    g = pidx // 2
    h = pidx % 2
    m = h * XS + x
    me = pidx * XS + x
    count = groups * GM
    per_owner = 32 // groups
    orow = per_owner * 32

    def at_member(mm):
        return (g * 2 + mm // XS, mm % XS)

    def at_group(gg):
        return (gg * 2 + h, x)

    def at_device(d):
        return (d // XS, d % XS)

    upper = at_device((me + 1) % count)
    lower = at_device((me + count - 1) % count)

    def remote(src, dst, ssem, rsem, dev):
        return pltpu.make_async_remote_copy(
            src_ref=src, dst_ref=dst, send_sem=ssem, recv_sem=rsem,
            device_id=dev, device_id_type=MESH,
        )

    loads = [
        pltpu.make_async_copy(res_hbm.at[i // 2, i % 2], res_v.at[:, pl.ds(256 * i, 256)], load_sem.at[i])
        for i in range(4)
    ]
    loads.append(pltpu.make_async_copy(basis_hbm, basis_v, load_sem.at[4]))
    loads.append(pltpu.make_async_copy(cinv_hbm, cinv_v, load_sem.at[5]))
    for copy in loads:
        copy.start()

    def inv_copy(i):
        return pltpu.make_async_copy(inv_hbm.at[i // 2, i % 2], inv_v.at[i], inv_sem.at[i])

    barrier = pltpu.get_barrier_semaphore()
    peers = [upper, lower]
    peers += [at_member((m + k) % GM) for k in range(1, GM)]
    peers += [at_group((g + k) % groups) for k in range(1, groups)]
    for dev in peers:
        pl.semaphore_signal(barrier, inc=1, device_id=dev, device_id_type=MESH)

    for b in range(2):
        row = send_ref[0, b : b + 1, :].astype(F32)
        col = columns(row)
        for t in range(NODE // 128):
            ss[128 * b : 128 * b + 128, 128 * t : 128 * t + 128] = hot(
                col == iota((128, 128), 1) + float(128 * t)
            )
        sst[:, 128 * b : 128 * b + 128] = hot(iota((NODE, 128), 0) == row)

    lane = lax.broadcasted_iota(jnp.int32, (8, 128), 1)
    target = jnp.where(
        lane < 64,
        jnp.where(lane < 32, cb_ref[0], cb_ref[1]),
        jnp.where(lane < 96, cb_ref[2], cb_ref[3]),
    ) * 32 + lane % 32
    cbt[...] = target.astype(F32)
    cbr[0] = target.astype(F32)

    def halo_out(b):
        return remote(
            hs1.at[pl.ds(128 * b, 128)], hr1.at[pl.ds(128 * b, 128)],
            hs_sem.at[b], hr_sem.at[b], upper if b == 0 else lower,
        )

    for i in range(4):
        loads[i].wait()
    for i in range(8):
        inv_copy(i).start()
    for b in range(2):
        here = slice(128 * b, 128 * b + 128)
        hs1[here] = dot(ss[here], res_v[...]).astype(BF16)
        if b == 0:
            pl.semaphore_wait(barrier, len(peers))
        halo_out(b).start()

    def cb_out(k):
        return remote(cbt, cbr.at[k], cb_ss.at[k], cb_rs.at[k], at_member((m + k) % GM))

    for k in range(1, GM):
        cb_out(k).start()
    loads[5].wait()
    first = 32 * h + per_owner * g
    holder = first // 16
    mine = cinv_v.at[pl.ds(first % 16, per_owner)]

    def ci_out(k):
        return remote(mine, ci_v, ci_ss.at[k], ci_rs, (pidx, (x + k) % XS))

    @pl.when(x == holder)
    def _():
        for k in range(1, XS):
            ci_out(k).start()
        ci_v[...] = cinv_v[pl.ds(first % 16, per_owner)]

    s = slots_ref[...].astype(F32)
    base = iota((4, PN), 0) * float(CORE)
    is_rem = s >= float(NODE)
    is_core = (s >= base) & (s < base + float(CORE))
    weight = jnp.where(is_rem, 256.0, jnp.where(is_core, 0.0, 1.0)).astype(BF16)
    tri = hot(iota((PN, PN), 0) < iota((PN, PN), 1))
    ranks = dot(weight, tri)
    rank_r = jnp.floor(ranks * (1.0 / 256.0))
    rank_o = ranks - 256.0 * rank_r
    place = jnp.where(is_core, s - base, jnp.where(is_rem, 448.0 + rank_r, 384.0 + rank_o))
    for p in range(4):
        krow_s[p] = place[p : p + 1, :]

    def build(p, carry):
        krow = krow_s[p]
        permt[p] = hot(iota((PN, PN), 0) == krow)
        for c in range(4):
            col = columns(krow[:, 128 * c : 128 * c + 128])
            for t in range(4):
                perm[p, 128 * c : 128 * c + 128, 128 * t : 128 * t + 128] = hot(
                    col == iota((128, 128), 1) + float(128 * t)
                )
        return carry

    lax.fori_loop(0, 4, build, 0)
    s_hi = jnp.floor(s * (1.0 / 128.0))
    s_lo = s - 128.0 * s_hi
    s_hi, s_lo = s_hi.astype(BF16), s_lo.astype(BF16)
    values = []
    for p in range(4):
        tail = perm[p, :, 384:512]
        values.append((128.0 * dot(s_hi, tail) + dot(s_lo, tail))[p : p + 1, :])
    low_lane = lax.broadcasted_iota(jnp.int32, (1, 128), 1) < 64
    for j in range(2):
        v0, v1 = values[2 * j], values[2 * j + 1]
        row_o = jnp.where(low_lane, v0, pltpu.roll(v1, 64, 1))
        row_r = jnp.where(low_lane, pltpu.roll(v0, 64, 1), v1) - float(NODE)
        here = slice(128 * j, 128 * j + 128)
        col = columns(row_o)
        for t in range(NODE // 128):
            sel_o[here, 128 * t : 128 * t + 128] = hot(
                col == iota((128, 128), 1) + float(128 * t)
            )
        sel_ot[:, here] = hot(iota((NODE, 128), 0) == row_o)
        col = columns(row_r)
        for t in range(2):
            sel_r[here, 128 * t : 128 * t + 128] = hot(
                col == iota((128, 128), 1) + float(128 * t)
            )
        sel_rt[:, here] = hot(iota((256, 128), 0) == row_r)

    others = dot(sel_o[...], res_v[...]).astype(BF16)
    for p in range(4):
        u[p, 0:CORE] = res_v[CORE * p : CORE * p + CORE]
        u[p, CORE : CORE + 64] = others[64 * p : 64 * p + 64]

    loads[4].wait()

    def bases(p, carry):
        rows = jnp.concatenate(
            [basis_v[p, i // 2, :, PN * (i % 2) : PN * (i % 2) + PN] for i in range(4)], axis=0
        )
        bp[p] = dot_t(permt[p], rows).astype(BF16)
        return carry

    lax.fori_loop(0, 4, bases, 0)
    cbig[...] = jnp.zeros_like(cbig)

    offset = (h * HALF).astype(F32)
    for k in range(GM):
        if k:
            cb_out(k).wait_recv()
        row = cbr[k, 0:1, :] - offset
        here = slice(128 * k, 128 * k + 128)
        oht[:, here] = hot(iota((HALF, 128), 0) == row)
        col = columns(row)
        for t in range(HALF // 128):
            oh[here, 128 * t : 128 * t + 128] = hot(col == iota((128, 128), 1) + float(128 * t))

    for b in range(2):
        halo_out(b).wait_recv()
    far = dot(sel_r[...], hr1[...]).astype(BF16)
    for p in range(4):
        u[p, CORE + 64 : PN] = far[64 * p : 64 * p + 64]

    def gather(p, carry):
        rows = dot(perm[p], u[p]).astype(BF16)
        for i in range(4):
            gath[p, i // 2, PN * (i % 2) : PN * (i % 2) + PN] = rows[:, 256 * i : 256 * i + 256]
        for w in range(2):
            part = dot(basis_v[p, w], gath[p, w]).astype(BF16)
            for e in range(2):
                sb1[2 * w + e, pl.ds(32 * p, 32)] = part[:, 128 * e : 128 * e + 128]
        return carry

    lax.fori_loop(0, 4, gather, 0)

    def stage_a(k):
        mm = (m + k) % GM
        return remote(sb1.at[mm % XS], xb.at[pl.ds(128 * k, 128)], a_ss.at[k], a_rs.at[k], at_member(mm))

    for k in range(1, GM):
        stage_a(k).start()
    xb[0:128] = sb1[x]

    def local(p, carry):
        for w in range(2):
            inv_copy(2 * p + w).wait()
            terms = dot(inv_v[2 * p + w], gath[p, w]).astype(BF16)
            for q in range(2):
                i = 2 * w + q
                u[p, :, 256 * i : 256 * i + 256] = terms[PN * q : PN * q + PN]
        y = dot(permt[p], u[p])
        own[pl.ds(pl.multiple_of(CORE * p, CORE), CORE)] = y[0:CORE]
        yor[p] = y[CORE:PN]
        return carry

    lax.fori_loop(0, 1, local, 0)

    for k in range(1, GM):
        stage_a(k).wait_recv()
    db[...] = dot(oht[...], xb[...]).astype(BF16)

    def stage_b(k):
        gg = (g + k) % groups
        return remote(
            db.at[pl.ds(pl.multiple_of(orow * gg, orow), orow)], s2.at[k],
            b_ss.at[k], b_rs.at[k], at_group(gg),
        )

    for k in range(1, groups):
        stage_b(k).start()

    lax.fori_loop(1, 3, local, 0)

    own_rows = pl.ds(pl.multiple_of(orow * g, orow), orow)
    total = db[own_rows].astype(F32)
    for k in range(1, groups):
        stage_b(k).wait_recv()
        total = total + s2[k].astype(F32)
    t_hi = total.astype(BF16)
    t_lo = (total - t_hi.astype(F32)).astype(BF16)

    @pl.when(x != holder)
    def _():
        ci_out(1).wait_recv()

    for b in range(per_owner):
        inv_b = ci_v[b, x // 2]
        rows = slice(32 * b, 32 * b + 32)
        cgs[rows] = (dot(inv_b, t_hi[rows]) + dot(inv_b, t_lo[rows])).astype(BF16)

    def stage_c(k):
        return remote(cgs, cg.at[own_rows], c_ss.at[k], c_rs.at[k], at_group((g + k) % groups))

    for k in range(1, groups):
        stage_c(k).start()
    cg[own_rows] = cgs[...]

    lax.fori_loop(3, 4, local, 0)

    for k in range(1, groups):
        stage_c(k).wait_recv()
    rb[...] = dot(oh[...], cg[...]).astype(BF16)

    def stage_d(k):
        return remote(
            rb.at[pl.ds(128 * k, 128)], cf.at[h, x], d_ss.at[k], d_rs.at[k],
            at_member((m + GM - k) % GM),
        )

    for k in range(1, GM):
        stage_d(k).start()
    cf[h, x] = rb[0:128]
    for k in range(1, GM):
        stage_d(k).wait_recv()

    for w in range(2):
        for e in range(2):
            both = cf[0, 2 * w + e] + cf[1, 2 * w + e]
            for p in range(4):
                for q in range(2):
                    i = 2 * w + q
                    cbig[p, 32 * i : 32 * i + 32, 256 * i + 128 * e : 256 * i + 128 * e + 128] = both[
                        32 * p : 32 * p + 32
                    ]
    for p in range(4):
        part = dot(bp[p, 448:512], cbig[p])
        yr[64 * p : 64 * p + 64] = (yor[p, 64:128] + part).astype(BF16)

    def back(b):
        return remote(
            hs2.at[pl.ds(128 * b, 128)], hr2.at[pl.ds(128 * b, 128)],
            hs2_sem.at[b], hr2_sem.at[b], lower if b == 0 else upper,
        )

    hs2[...] = dot(sel_rt[...], yr[...]).astype(BF16)
    for b in range(2):
        back(b).start()

    def coarse_own(p, carry):
        rows = pl.ds(pl.multiple_of(CORE * p, CORE), CORE)
        part = dot(bp[p, 0:448], cbig[p])
        own[rows] += part[0:CORE]
        yo[pl.ds(pl.multiple_of(64 * p, 64), 64)] = (yor[p, 0:64] + part[CORE:448]).astype(BF16)
        return carry

    lax.fori_loop(0, 4, coarse_own, 0)

    def spread(t, carry):
        rows = pl.ds(pl.multiple_of(CORE * t, CORE), CORE)
        own[rows] += dot(sel_ot[rows], yo[...])
        return carry

    lax.fori_loop(0, 4, spread, 0)

    for b in range(2):
        back(b).wait_recv()

    def finish(t, carry):
        rows = pl.ds(pl.multiple_of(CORE * t, CORE), CORE)
        block = (own[rows] + dot(sst[rows], hr2[...])).astype(BF16)
        for i in range(4):
            out_ref[i // 2, i % 2, rows] = block[:, 256 * i : 256 * i + 256]
        return carry

    lax.fori_loop(0, 4, finish, 0)

    for b in range(2):
        halo_out(b).wait_send()
        back(b).wait_send()
    for k in range(1, GM):
        cb_out(k).wait_send()
        stage_a(k).wait_send()
        stage_d(k).wait_send()
    for k in range(1, groups):
        stage_b(k).wait_send()
        stage_c(k).wait_send()

    @pl.when(x == holder)
    def _():
        for k in range(1, XS):
            ci_out(k).wait_send()


def solution(mesh):
    groups = mesh.shape["patch"] // 2
    per_owner = 32 // groups
    vm = pltpu.VMEM
    dma = pltpu.SemaphoreType.DMA
    scratch = [
        vm((NODE, 1024), BF16), vm((8, 1024, 1024), BF16), vm((4, 2, 32, 1024), BF16),
        vm((16, 2, 32, 32), BF16), vm((per_owner, 2, 32, 32), BF16),
        vm((4, 1, PN), F32),
        vm((256, NODE), BF16), vm((NODE, 256), BF16),
        vm((256, NODE), BF16), vm((NODE, 256), BF16),
        vm((256, 256), BF16), vm((256, 256), BF16),
        vm((4, PN, PN), BF16), vm((4, PN, PN), BF16),
        vm((256, 1024), BF16), vm((256, 1024), BF16),
        vm((256, 1024), BF16), vm((256, 1024), BF16),
        vm((4, PN, 1024), BF16), vm((4, 2, 1024, 256), BF16),
        vm((4, PN, 128), BF16), vm((4, 128, 1024), BF16),
        vm((NODE, 1024), F32), vm((4, 128, 1024), F32),
        vm((256, 1024), BF16), vm((256, 1024), BF16),
        vm((8, 128), F32), vm((GM, 8, 128), F32),
        vm((HALF, HALF), BF16), vm((HALF, HALF), BF16),
        vm((4, 128, 128), BF16), vm((HALF, 128), BF16), vm((HALF, 128), BF16),
        vm((groups, 32 * per_owner, 128), BF16), vm((32 * per_owner, 128), BF16),
        vm((HALF, 128), BF16), vm((HALF, 128), BF16), vm((2, 4, 128, 128), BF16),
        dma((6,)), dma((8,)), dma((2,)), dma((2,)), dma((2,)), dma((2,)),
        dma((GM,)), dma((GM,)), dma((XS,)), dma,
        dma((GM,)), dma((GM,)), dma((groups,)), dma((groups,)),
        dma((groups,)), dma((groups,)), dma((GM,)), dma((GM,)),
    ]

    def per_device(residual, patch_inv, coarse_basis, coarse_inv, patch_slots, send_rows, coarse_block):
        hbm = pl.BlockSpec(memory_space=pl.ANY)
        vmem = pl.BlockSpec(memory_space=pltpu.VMEM)
        return pl.pallas_call(
            functools.partial(kernel, groups),
            out_shape=jax.ShapeDtypeStruct(residual.shape, BF16),
            in_specs=[hbm, hbm, hbm, hbm, vmem, vmem, pl.BlockSpec(memory_space=pltpu.SMEM)],
            out_specs=vmem,
            scratch_shapes=scratch,
            compiler_params=pltpu.CompilerParams(
                collective_id=0, has_side_effects=True, vmem_limit_bytes=62 * 1024 * 1024
            ),
        )(residual, patch_inv, jnp.swapaxes(coarse_basis, 2, 3), coarse_inv, patch_slots, send_rows, coarse_block)

    node = P(None, None, ("patch", "coarse"), None)
    both = ("patch", "coarse")
    return jax.shard_map(
        per_device,
        mesh=mesh,
        in_specs=(
            node, P(both, None, None, None), P(both, None, None, None),
            P("coarse", None, None, None), P(both, None), P(both, None, None), P(both),
        ),
        out_specs=node,
        check_vma=False,
    )
```

```python
import functools

import jax
import jax.numpy as jnp
from jax import lax
from jax.experimental import pallas as pl
from jax.experimental.pallas import tpu as pltpu
from jax.sharding import PartitionSpec as P

MESH = pl.DeviceIdType.MESH
F32 = jnp.float32
BF16 = jnp.bfloat16
NODE = 1536
CORE = 384
PN = 512
XS = 4
GM = 8
HALF = 1024


def dot(a, b):
    return lax.dot_general(a, b, (((1,), (0,)), ((), ())), preferred_element_type=F32)


def dot_t(a, b):
    return lax.dot_general(a, b, (((1,), (1,)), ((), ())), preferred_element_type=F32)


def iota(shape, axis):
    return lax.broadcasted_iota(jnp.int32, shape, axis).astype(F32)


def hot(mask):
    return jnp.where(mask, 1.0, 0.0).astype(BF16)


def columns(row):
    return jnp.transpose(jnp.broadcast_to(row, (128, 128)))


def kernel(
    groups,
    res_hbm, inv_hbm, basis_hbm, cinv_hbm, slots_ref, send_ref, cb_ref,
    own_hbm, far_ref,
    res_v, inv_v, basis_v, cinv_v, ci_v,
    krow_s, ss, sel_o, sel_ot, sel_r, sel_rt, perm, permt,
    hs1, hr1, hs2, hr2, u, gath, bp, cbig, own, yor, yo, yr,
    cbt, cbr, oh, oht, sb1, xb, db, s2, cgs, cg, rb, cf,
    load_sem, inv_sem, hs_sem, hr_sem, hs2_sem, hr2_sem,
    cb_ss, cb_rs, ci_ss, ci_rs, a_ss, a_rs, b_ss, b_rs, c_ss, c_rs, d_ss, d_rs,
):
    pidx = lax.axis_index("patch")
    x = lax.axis_index("coarse")
    g = pidx // 2
    h = pidx % 2
    m = h * XS + x
    me = pidx * XS + x
    count = groups * GM
    per_owner = 32 // groups
    orow = per_owner * 32

    def at_member(mm):
        return (g * 2 + mm // XS, mm % XS)

    def at_group(gg):
        return (gg * 2 + h, x)

    def at_device(d):
        return (d // XS, d % XS)

    upper = at_device((me + 1) % count)
    lower = at_device((me + count - 1) % count)

    def remote(src, dst, ssem, rsem, dev):
        return pltpu.make_async_remote_copy(
            src_ref=src, dst_ref=dst, send_sem=ssem, recv_sem=rsem,
            device_id=dev, device_id_type=MESH,
        )

    loads = [
        pltpu.make_async_copy(res_hbm.at[i // 2, i % 2], res_v.at[:, pl.ds(256 * i, 256)], load_sem.at[i])
        for i in range(4)
    ]
    loads.append(pltpu.make_async_copy(basis_hbm, basis_v, load_sem.at[4]))
    loads.append(pltpu.make_async_copy(cinv_hbm, cinv_v, load_sem.at[5]))
    for copy in loads:
        copy.start()

    def inv_copy(i):
        return pltpu.make_async_copy(inv_hbm.at[i // 2, i % 2], inv_v.at[i], inv_sem.at[i])

    barrier = pltpu.get_barrier_semaphore()
    peers = [upper, lower]
    peers += [at_member((m + k) % GM) for k in range(1, GM)]
    peers += [at_group((g + k) % groups) for k in range(1, groups)]
    for dev in peers:
        pl.semaphore_signal(barrier, inc=1, device_id=dev, device_id_type=MESH)

    for b in range(2):
        row = send_ref[0, b : b + 1, :].astype(F32)
        col = columns(row)
        for t in range(NODE // 128):
            ss[128 * b : 128 * b + 128, 128 * t : 128 * t + 128] = hot(
                col == iota((128, 128), 1) + float(128 * t)
            )

    lane = lax.broadcasted_iota(jnp.int32, (8, 128), 1)
    target = jnp.where(
        lane < 64,
        jnp.where(lane < 32, cb_ref[0], cb_ref[1]),
        jnp.where(lane < 96, cb_ref[2], cb_ref[3]),
    ) * 32 + lane % 32
    cbt[...] = target.astype(F32)
    cbr[0] = target.astype(F32)

    def halo_out(b):
        return remote(
            hs1.at[pl.ds(128 * b, 128)], hr1.at[pl.ds(128 * b, 128)],
            hs_sem.at[b], hr_sem.at[b], upper if b == 0 else lower,
        )

    for i in range(4):
        loads[i].wait()
    for i in range(8):
        inv_copy(i).start()
    for b in range(2):
        here = slice(128 * b, 128 * b + 128)
        hs1[here] = dot(ss[here], res_v[...]).astype(BF16)
        if b == 0:
            pl.semaphore_wait(barrier, len(peers))
        halo_out(b).start()

    def cb_out(k):
        return remote(cbt, cbr.at[k], cb_ss.at[k], cb_rs.at[k], at_member((m + k) % GM))

    for k in range(1, GM):
        cb_out(k).start()
    loads[5].wait()
    first = 32 * h + per_owner * g
    holder = first // 16
    mine = cinv_v.at[pl.ds(first % 16, per_owner)]

    def ci_out(k):
        return remote(mine, ci_v, ci_ss.at[k], ci_rs, (pidx, (x + k) % XS))

    @pl.when(x == holder)
    def _():
        for k in range(1, XS):
            ci_out(k).start()
        ci_v[...] = cinv_v[pl.ds(first % 16, per_owner)]

    s = slots_ref[...].astype(F32)
    base = iota((4, PN), 0) * float(CORE)
    is_rem = s >= float(NODE)
    is_core = (s >= base) & (s < base + float(CORE))
    weight = jnp.where(is_rem, 256.0, jnp.where(is_core, 0.0, 1.0)).astype(BF16)
    tri = hot(iota((PN, PN), 0) < iota((PN, PN), 1))
    ranks = dot(weight, tri)
    rank_r = jnp.floor(ranks * (1.0 / 256.0))
    rank_o = ranks - 256.0 * rank_r
    place = jnp.where(is_core, s - base, jnp.where(is_rem, 448.0 + rank_r, 384.0 + rank_o))
    for p in range(4):
        krow_s[p] = place[p : p + 1, :]

    def build(p, carry):
        krow = krow_s[p]
        permt[p] = hot(iota((PN, PN), 0) == krow)
        for c in range(4):
            col = columns(krow[:, 128 * c : 128 * c + 128])
            for t in range(4):
                perm[p, 128 * c : 128 * c + 128, 128 * t : 128 * t + 128] = hot(
                    col == iota((128, 128), 1) + float(128 * t)
                )
        return carry

    lax.fori_loop(0, 4, build, 0)
    s_hi = jnp.floor(s * (1.0 / 128.0))
    s_lo = s - 128.0 * s_hi
    s_hi, s_lo = s_hi.astype(BF16), s_lo.astype(BF16)
    values = []
    for p in range(4):
        tail = perm[p, :, 384:512]
        values.append((128.0 * dot(s_hi, tail) + dot(s_lo, tail))[p : p + 1, :])
    low_lane = lax.broadcasted_iota(jnp.int32, (1, 128), 1) < 64
    for j in range(2):
        v0, v1 = values[2 * j], values[2 * j + 1]
        row_o = jnp.where(low_lane, v0, pltpu.roll(v1, 64, 1))
        row_r = jnp.where(low_lane, pltpu.roll(v0, 64, 1), v1) - float(NODE)
        here = slice(128 * j, 128 * j + 128)
        col = columns(row_o)
        for t in range(NODE // 128):
            sel_o[here, 128 * t : 128 * t + 128] = hot(
                col == iota((128, 128), 1) + float(128 * t)
            )
        sel_ot[:, here] = hot(iota((NODE, 128), 0) == row_o)
        col = columns(row_r)
        for t in range(2):
            sel_r[here, 128 * t : 128 * t + 128] = hot(
                col == iota((128, 128), 1) + float(128 * t)
            )
        sel_rt[:, here] = hot(iota((256, 128), 0) == row_r)

    others = dot(sel_o[...], res_v[...]).astype(BF16)
    for p in range(4):
        u[p, 0:CORE] = res_v[CORE * p : CORE * p + CORE]
        u[p, CORE : CORE + 64] = others[64 * p : 64 * p + 64]

    loads[4].wait()

    def bases(p, carry):
        rows = jnp.concatenate(
            [basis_v[p, i // 2, :, PN * (i % 2) : PN * (i % 2) + PN] for i in range(4)], axis=0
        )
        bp[p] = dot_t(permt[p], rows).astype(BF16)
        return carry

    lax.fori_loop(0, 4, bases, 0)
    cbig[...] = jnp.zeros_like(cbig)

    offset = (h * HALF).astype(F32)
    for k in range(GM):
        if k:
            cb_out(k).wait_recv()
        row = cbr[k, 0:1, :] - offset
        here = slice(128 * k, 128 * k + 128)
        oht[:, here] = hot(iota((HALF, 128), 0) == row)
        col = columns(row)
        for t in range(HALF // 128):
            oh[here, 128 * t : 128 * t + 128] = hot(col == iota((128, 128), 1) + float(128 * t))

    for b in range(2):
        halo_out(b).wait_recv()
    far = dot(sel_r[...], hr1[...]).astype(BF16)
    for p in range(4):
        u[p, CORE + 64 : PN] = far[64 * p : 64 * p + 64]

    def gather(p, carry):
        rows = dot(perm[p], u[p]).astype(BF16)
        for i in range(4):
            gath[p, i // 2, PN * (i % 2) : PN * (i % 2) + PN] = rows[:, 256 * i : 256 * i + 256]
        for w in range(2):
            part = dot(basis_v[p, w], gath[p, w]).astype(BF16)
            for e in range(2):
                sb1[2 * w + e, pl.ds(32 * p, 32)] = part[:, 128 * e : 128 * e + 128]
        return carry

    lax.fori_loop(0, 4, gather, 0)

    def stage_a(k):
        mm = (m + k) % GM
        return remote(sb1.at[mm % XS], xb.at[pl.ds(128 * k, 128)], a_ss.at[k], a_rs.at[k], at_member(mm))

    for k in range(1, GM):
        stage_a(k).start()
    xb[0:128] = sb1[x]

    def local(p, carry):
        for w in range(2):
            inv_copy(2 * p + w).wait()
            terms = dot(inv_v[2 * p + w], gath[p, w]).astype(BF16)
            for q in range(2):
                i = 2 * w + q
                u[p, :, 256 * i : 256 * i + 256] = terms[PN * q : PN * q + PN]
        y = dot(permt[p], u[p])
        own[pl.ds(pl.multiple_of(CORE * p, CORE), CORE)] = y[0:CORE]
        yor[p] = y[CORE:PN]
        return carry

    lax.fori_loop(0, 1, local, 0)

    for k in range(1, GM):
        stage_a(k).wait_recv()
    db[...] = dot(oht[...], xb[...]).astype(BF16)

    def stage_b(k):
        gg = (g + k) % groups
        return remote(
            db.at[pl.ds(pl.multiple_of(orow * gg, orow), orow)], s2.at[k],
            b_ss.at[k], b_rs.at[k], at_group(gg),
        )

    for k in range(1, groups):
        stage_b(k).start()

    lax.fori_loop(1, 3, local, 0)

    own_rows = pl.ds(pl.multiple_of(orow * g, orow), orow)
    total = db[own_rows].astype(F32)
    for k in range(1, groups):
        stage_b(k).wait_recv()
        total = total + s2[k].astype(F32)
    t_hi = total.astype(BF16)
    t_lo = (total - t_hi.astype(F32)).astype(BF16)

    @pl.when(x != holder)
    def _():
        ci_out(1).wait_recv()

    for b in range(per_owner):
        inv_b = ci_v[b, x // 2]
        rows = slice(32 * b, 32 * b + 32)
        cgs[rows] = (dot(inv_b, t_hi[rows]) + dot(inv_b, t_lo[rows])).astype(BF16)

    def stage_c(k):
        return remote(cgs, cg.at[own_rows], c_ss.at[k], c_rs.at[k], at_group((g + k) % groups))

    for k in range(1, groups):
        stage_c(k).start()
    cg[own_rows] = cgs[...]

    lax.fori_loop(3, 4, local, 0)

    for k in range(1, groups):
        stage_c(k).wait_recv()
    rb[...] = dot(oh[...], cg[...]).astype(BF16)

    def stage_d(k):
        return remote(
            rb.at[pl.ds(128 * k, 128)], cf.at[h, x], d_ss.at[k], d_rs.at[k],
            at_member((m + GM - k) % GM),
        )

    for k in range(1, GM):
        stage_d(k).start()
    cf[h, x] = rb[0:128]
    for k in range(1, GM):
        stage_d(k).wait_recv()

    for w in range(2):
        for e in range(2):
            both = cf[0, 2 * w + e] + cf[1, 2 * w + e]
            for p in range(4):
                for q in range(2):
                    i = 2 * w + q
                    cbig[p, 32 * i : 32 * i + 32, 256 * i + 128 * e : 256 * i + 128 * e + 128] = both[
                        32 * p : 32 * p + 32
                    ]
    for p in range(4):
        part = dot(bp[p, 448:512], cbig[p])
        yr[64 * p : 64 * p + 64] = (yor[p, 64:128] + part).astype(BF16)

    def back(b):
        return remote(
            hs2.at[pl.ds(128 * b, 128)], hr2.at[pl.ds(128 * b, 128)],
            hs2_sem.at[b], hr2_sem.at[b], lower if b == 0 else upper,
        )

    hs2[...] = dot(sel_rt[...], yr[...]).astype(BF16)
    for b in range(2):
        back(b).start()

    def coarse_own(p, carry):
        rows = pl.ds(pl.multiple_of(CORE * p, CORE), CORE)
        part = dot(bp[p, 0:448], cbig[p])
        own[rows] += part[0:CORE]
        yo[pl.ds(pl.multiple_of(64 * p, 64), 64)] = (yor[p, 0:64] + part[CORE:448]).astype(BF16)
        return carry

    lax.fori_loop(0, 4, coarse_own, 0)

    def spread(t, carry):
        rows = pl.ds(pl.multiple_of(CORE * t, CORE), CORE)
        res_v[rows] = (own[rows] + dot(sel_ot[rows], yo[...])).astype(BF16)
        return carry

    lax.fori_loop(0, 4, spread, 0)

    stores = [
        pltpu.make_async_copy(
            res_v.at[:, pl.ds(256 * i, 256)], own_hbm.at[i // 2, i % 2], load_sem.at[i]
        )
        for i in range(4)
    ]
    for copy in stores:
        copy.start()
    for b in range(2):
        back(b).wait_recv()
    far_ref[...] = hr2[...]
    for copy in stores:
        copy.wait()

    for b in range(2):
        halo_out(b).wait_send()
        back(b).wait_send()
    for k in range(1, GM):
        cb_out(k).wait_send()
        stage_a(k).wait_send()
        stage_d(k).wait_send()
    for k in range(1, groups):
        stage_b(k).wait_send()
        stage_c(k).wait_send()

    @pl.when(x == holder)
    def _():
        for k in range(1, XS):
            ci_out(k).wait_send()


def add_far(send_ref, own_ref, far_ref, out_ref):
    rows = own_ref.shape[2]
    ids = iota((rows, 128), 0) + (pl.program_id(0) * rows).astype(F32)
    maps = [hot(ids == send_ref[0, b : b + 1, :].astype(F32)) for b in range(2)]
    added = dot(jnp.concatenate(maps, axis=1), far_ref[...])
    for i in range(4):
        out_ref[i // 2, i % 2] = (
            own_ref[i // 2, i % 2].astype(F32) + added[:, 256 * i : 256 * i + 256]
        ).astype(BF16)


def solution(mesh):
    groups = mesh.shape["patch"] // 2
    per_owner = 32 // groups
    vm = pltpu.VMEM
    dma = pltpu.SemaphoreType.DMA
    scratch = [
        vm((NODE, 1024), BF16), vm((8, 1024, 1024), BF16), vm((4, 2, 32, 1024), BF16),
        vm((16, 2, 32, 32), BF16), vm((per_owner, 2, 32, 32), BF16),
        vm((4, 1, PN), F32),
        vm((256, NODE), BF16),
        vm((256, NODE), BF16), vm((NODE, 256), BF16),
        vm((256, 256), BF16), vm((256, 256), BF16),
        vm((4, PN, PN), BF16), vm((4, PN, PN), BF16),
        vm((256, 1024), BF16), vm((256, 1024), BF16),
        vm((256, 1024), BF16), vm((256, 1024), BF16),
        vm((4, PN, 1024), BF16), vm((4, 2, 1024, 256), BF16),
        vm((4, PN, 128), BF16), vm((4, 128, 1024), BF16),
        vm((NODE, 1024), F32), vm((4, 128, 1024), F32),
        vm((256, 1024), BF16), vm((256, 1024), BF16),
        vm((8, 128), F32), vm((GM, 8, 128), F32),
        vm((HALF, HALF), BF16), vm((HALF, HALF), BF16),
        vm((4, 128, 128), BF16), vm((HALF, 128), BF16), vm((HALF, 128), BF16),
        vm((groups, 32 * per_owner, 128), BF16), vm((32 * per_owner, 128), BF16),
        vm((HALF, 128), BF16), vm((HALF, 128), BF16), vm((2, 4, 128, 128), BF16),
        dma((6,)), dma((8,)), dma((2,)), dma((2,)), dma((2,)), dma((2,)),
        dma((GM,)), dma((GM,)), dma((XS,)), dma,
        dma((GM,)), dma((GM,)), dma((groups,)), dma((groups,)),
        dma((groups,)), dma((groups,)), dma((GM,)), dma((GM,)),
    ]

    def per_device(residual, patch_inv, coarse_basis, coarse_inv, patch_slots, send_rows, coarse_block):
        hbm = pl.BlockSpec(memory_space=pl.ANY)
        vmem = pl.BlockSpec(memory_space=pltpu.VMEM)
        own, far = pl.pallas_call(
            functools.partial(kernel, groups),
            out_shape=(
                jax.ShapeDtypeStruct(residual.shape, BF16),
                jax.ShapeDtypeStruct((256, 1024), BF16),
            ),
            in_specs=[hbm, hbm, hbm, hbm, vmem, vmem, pl.BlockSpec(memory_space=pltpu.SMEM)],
            out_specs=(hbm, vmem),
            scratch_shapes=scratch,
            compiler_params=pltpu.CompilerParams(
                collective_id=0, has_side_effects=True, vmem_limit_bytes=62 * 1024 * 1024
            ),
        )(residual, patch_inv, jnp.swapaxes(coarse_basis, 2, 3), coarse_inv, patch_slots, send_rows, coarse_block)
        part = pl.BlockSpec((2, 2, CORE, 256), lambda t: (0, 0, t, 0))
        return pl.pallas_call(
            add_far,
            grid=(NODE // CORE,),
            out_shape=jax.ShapeDtypeStruct(residual.shape, BF16),
            in_specs=[
                pl.BlockSpec((1, 2, 128), lambda t: (0, 0, 0)),
                part,
                pl.BlockSpec((256, 1024), lambda t: (0, 0)),
            ],
            out_specs=part,
            compiler_params=pltpu.CompilerParams(vmem_limit_bytes=32 * 1024 * 1024),
        )(send_rows, own, far)

    node = P(None, None, ("patch", "coarse"), None)
    both = ("patch", "coarse")
    return jax.shard_map(
        per_device,
        mesh=mesh,
        in_specs=(
            node, P(both, None, None, None), P(both, None, None, None),
            P("coarse", None, None, None), P(both, None), P(both, None, None), P(both),
        ),
        out_specs=node,
        check_vma=False,
    )
```

```python
import functools

import jax
import jax.numpy as jnp
from jax import lax
from jax.experimental import pallas as pl
from jax.experimental.pallas import tpu as pltpu
from jax.sharding import PartitionSpec as P

MESH = pl.DeviceIdType.MESH
F32 = jnp.float32
BF16 = jnp.bfloat16
NODE = 1536
CORE = 384
PN = 512
XS = 4
GM = 8
HALF = 1024


def dot(a, b):
    return lax.dot_general(a, b, (((1,), (0,)), ((), ())), preferred_element_type=F32)


def dot_t(a, b):
    return lax.dot_general(a, b, (((1,), (1,)), ((), ())), preferred_element_type=F32)


def iota(shape, axis):
    return lax.broadcasted_iota(jnp.int32, shape, axis).astype(F32)


def hot(mask):
    return jnp.where(mask, 1.0, 0.0).astype(BF16)


def columns(row):
    return jnp.transpose(jnp.broadcast_to(row, (128, 128)))


def kernel(
    groups,
    res_hbm, inv_hbm, basis_hbm, cinv_hbm, slots_ref, send_ref, cb_ref,
    out_ref,
    res_v, inv_v, basis_v, cinv_v, ci_v,
    krow_s, ss, sst, sel_o, sel_ot, sel_r, sel_rt, perm, permt,
    hs1, hr1, hs2, hr2, u, gath, bp, bpt, cbig, own, yor, yo, yr,
    cbt, cbr, oh, oht, sb1, xb, db, s2, cgs, cg, rb, cf,
    load_sem, inv_sem, hs_sem, hr_sem, hs2_sem, hr2_sem,
    cb_ss, cb_rs, ci_ss, ci_rs, a_ss, a_rs, b_ss, b_rs, c_ss, c_rs, d_ss, d_rs,
):
    pidx = lax.axis_index("patch")
    x = lax.axis_index("coarse")
    g = pidx // 2
    h = pidx % 2
    m = h * XS + x
    me = pidx * XS + x
    count = groups * GM
    per_owner = 32 // groups
    orow = per_owner * 32

    def at_member(mm):
        return (g * 2 + mm // XS, mm % XS)

    def at_group(gg):
        return (gg * 2 + h, x)

    def at_device(d):
        return (d // XS, d % XS)

    upper = at_device((me + 1) % count)
    lower = at_device((me + count - 1) % count)

    def remote(src, dst, ssem, rsem, dev):
        return pltpu.make_async_remote_copy(
            src_ref=src, dst_ref=dst, send_sem=ssem, recv_sem=rsem,
            device_id=dev, device_id_type=MESH,
        )

    loads = [
        pltpu.make_async_copy(res_hbm.at[i // 2, i % 2], res_v.at[:, pl.ds(256 * i, 256)], load_sem.at[i])
        for i in range(4)
    ]
    loads.append(pltpu.make_async_copy(basis_hbm, basis_v, load_sem.at[4]))
    loads.append(pltpu.make_async_copy(cinv_hbm, cinv_v, load_sem.at[5]))
    for copy in loads:
        copy.start()

    def inv_copy(i):
        return pltpu.make_async_copy(inv_hbm.at[i // 2, i % 2], inv_v.at[i], inv_sem.at[i])

    barrier = pltpu.get_barrier_semaphore()
    peers = [upper, lower]
    peers += [at_member((m + k) % GM) for k in range(1, GM)]
    peers += [at_group((g + k) % groups) for k in range(1, groups)]
    for dev in peers:
        pl.semaphore_signal(barrier, inc=1, device_id=dev, device_id_type=MESH)

    for b in range(2):
        row = send_ref[0, b : b + 1, :].astype(F32)
        col = columns(row)
        for t in range(NODE // 128):
            ss[128 * b : 128 * b + 128, 128 * t : 128 * t + 128] = hot(
                col == iota((128, 128), 1) + float(128 * t)
            )
        sst[:, 128 * b : 128 * b + 128] = hot(iota((NODE, 128), 0) == row)

    lane = lax.broadcasted_iota(jnp.int32, (8, 128), 1)
    target = jnp.where(
        lane < 64,
        jnp.where(lane < 32, cb_ref[0], cb_ref[1]),
        jnp.where(lane < 96, cb_ref[2], cb_ref[3]),
    ) * 32 + lane % 32
    cbt[...] = target.astype(F32)
    cbr[0] = target.astype(F32)

    def halo_out(b):
        return remote(
            hs1.at[pl.ds(128 * b, 128)], hr1.at[pl.ds(128 * b, 128)],
            hs_sem.at[b], hr_sem.at[b], upper if b == 0 else lower,
        )

    for i in range(4):
        loads[i].wait()
    for b in range(2):
        here = slice(128 * b, 128 * b + 128)
        hs1[here] = dot(ss[here], res_v[...]).astype(BF16)
        if b == 0:
            pl.semaphore_wait(barrier, len(peers))
        halo_out(b).start()

    def cb_out(k):
        return remote(cbt, cbr.at[k], cb_ss.at[k], cb_rs.at[k], at_member((m + k) % GM))

    for k in range(1, GM):
        cb_out(k).start()
    loads[5].wait()
    first = 32 * h + per_owner * g
    holder = first // 16
    mine = cinv_v.at[pl.ds(first % 16, per_owner)]

    def ci_out(k):
        return remote(mine, ci_v, ci_ss.at[k], ci_rs, (pidx, (x + k) % XS))

    @pl.when(x == holder)
    def _():
        for k in range(1, XS):
            ci_out(k).start()
        ci_v[...] = cinv_v[pl.ds(first % 16, per_owner)]

    s = slots_ref[...].astype(F32)
    base = iota((4, PN), 0) * float(CORE)
    is_rem = s >= float(NODE)
    is_core = (s >= base) & (s < base + float(CORE))
    weight = jnp.where(is_rem, 256.0, jnp.where(is_core, 0.0, 1.0)).astype(BF16)
    tri = hot(iota((PN, PN), 0) < iota((PN, PN), 1))
    ranks = dot(weight, tri)
    rank_r = jnp.floor(ranks * (1.0 / 256.0))
    rank_o = ranks - 256.0 * rank_r
    place = jnp.where(is_core, s - base, jnp.where(is_rem, 448.0 + rank_r, 384.0 + rank_o))
    for p in range(4):
        krow_s[p] = place[p : p + 1, :]

    def build(p, carry):
        krow = krow_s[p]
        permt[p] = hot(iota((PN, PN), 0) == krow)
        for c in range(4):
            col = columns(krow[:, 128 * c : 128 * c + 128])
            for t in range(4):
                perm[p, 128 * c : 128 * c + 128, 128 * t : 128 * t + 128] = hot(
                    col == iota((128, 128), 1) + float(128 * t)
                )
        return carry

    lax.fori_loop(0, 4, build, 0)
    s_hi = jnp.floor(s * (1.0 / 128.0))
    s_lo = s - 128.0 * s_hi
    s_hi, s_lo = s_hi.astype(BF16), s_lo.astype(BF16)
    values = []
    for p in range(4):
        tail = perm[p, :, 384:512]
        values.append((128.0 * dot(s_hi, tail) + dot(s_lo, tail))[p : p + 1, :])
    low_lane = lax.broadcasted_iota(jnp.int32, (1, 128), 1) < 64
    for j in range(2):
        v0, v1 = values[2 * j], values[2 * j + 1]
        row_o = jnp.where(low_lane, v0, pltpu.roll(v1, 64, 1))
        row_r = jnp.where(low_lane, pltpu.roll(v0, 64, 1), v1) - float(NODE)
        here = slice(128 * j, 128 * j + 128)
        col = columns(row_o)
        for t in range(NODE // 128):
            sel_o[here, 128 * t : 128 * t + 128] = hot(
                col == iota((128, 128), 1) + float(128 * t)
            )
        sel_ot[:, here] = hot(iota((NODE, 128), 0) == row_o)
        col = columns(row_r)
        for t in range(2):
            sel_r[here, 128 * t : 128 * t + 128] = hot(
                col == iota((128, 128), 1) + float(128 * t)
            )
        sel_rt[:, here] = hot(iota((256, 128), 0) == row_r)

    others = dot(sel_o[...], res_v[...]).astype(BF16)
    for p in range(4):
        u[p, 0:CORE] = res_v[CORE * p : CORE * p + CORE]
        u[p, CORE : CORE + 64] = others[64 * p : 64 * p + 64]

    loads[4].wait()

    def bases(p, carry):
        rows = jnp.concatenate(
            [basis_v[p, i // 2, :, PN * (i % 2) : PN * (i % 2) + PN] for i in range(4)], axis=0
        )
        bp[p] = dot_t(permt[p], rows).astype(BF16)
        bpt[p] = dot(rows, perm[p]).astype(BF16)
        return carry

    lax.fori_loop(0, 4, bases, 0)
    cbig[...] = jnp.zeros_like(cbig)

    offset = (h * HALF).astype(F32)
    for k in range(GM):
        if k:
            cb_out(k).wait_recv()
        row = cbr[k, 0:1, :] - offset
        here = slice(128 * k, 128 * k + 128)
        oht[:, here] = hot(iota((HALF, 128), 0) == row)
        col = columns(row)
        for t in range(HALF // 128):
            oh[here, 128 * t : 128 * t + 128] = hot(col == iota((128, 128), 1) + float(128 * t))

    for b in range(2):
        halo_out(b).wait_recv()
    for i in range(8):
        inv_copy(i).start()
    far = dot(sel_r[...], hr1[...]).astype(BF16)
    for p in range(4):
        u[p, CORE + 64 : PN] = far[64 * p : 64 * p + 64]

    def restrict(p, carry):
        full = dot(bpt[p], u[p])
        for w in range(2):
            part = full[64 * w : 64 * w + 32, 512 * w : 512 * w + 256]
            part = part + full[64 * w + 32 : 64 * w + 64, 512 * w + 256 : 512 * w + 512]
            part = part.astype(BF16)
            for e in range(2):
                sb1[2 * w + e, pl.ds(32 * p, 32)] = part[:, 128 * e : 128 * e + 128]
        return carry

    lax.fori_loop(0, 4, restrict, 0)

    def stage_a(k):
        mm = (m + k) % GM
        return remote(sb1.at[mm % XS], xb.at[pl.ds(128 * k, 128)], a_ss.at[k], a_rs.at[k], at_member(mm))

    for k in range(1, GM):
        stage_a(k).start()
    xb[0:128] = sb1[x]

    def gather(p, carry):
        rows = dot(perm[p], u[p]).astype(BF16)
        for i in range(4):
            gath[p, i // 2, PN * (i % 2) : PN * (i % 2) + PN] = rows[:, 256 * i : 256 * i + 256]
        return carry

    lax.fori_loop(0, 4, gather, 0)

    def local(p, carry):
        for w in range(2):
            inv_copy(2 * p + w).wait()
            terms = dot(inv_v[2 * p + w], gath[p, w]).astype(BF16)
            for q in range(2):
                i = 2 * w + q
                u[p, :, 256 * i : 256 * i + 256] = terms[PN * q : PN * q + PN]
        y = dot(permt[p], u[p])
        own[pl.ds(pl.multiple_of(CORE * p, CORE), CORE)] = y[0:CORE]
        yor[p] = y[CORE:PN]
        return carry

    for k in range(1, GM):
        stage_a(k).wait_recv()
    db[...] = dot(oht[...], xb[...]).astype(BF16)

    def stage_b(k):
        gg = (g + k) % groups
        return remote(
            db.at[pl.ds(pl.multiple_of(orow * gg, orow), orow)], s2.at[k],
            b_ss.at[k], b_rs.at[k], at_group(gg),
        )

    for k in range(1, groups):
        stage_b(k).start()

    lax.fori_loop(0, 2, local, 0)

    own_rows = pl.ds(pl.multiple_of(orow * g, orow), orow)
    total = db[own_rows].astype(F32)
    for k in range(1, groups):
        stage_b(k).wait_recv()
        total = total + s2[k].astype(F32)
    t_hi = total.astype(BF16)
    t_lo = (total - t_hi.astype(F32)).astype(BF16)

    @pl.when(x != holder)
    def _():
        ci_out(1).wait_recv()

    for b in range(per_owner):
        inv_b = ci_v[b, x // 2]
        rows = slice(32 * b, 32 * b + 32)
        cgs[rows] = (dot(inv_b, t_hi[rows]) + dot(inv_b, t_lo[rows])).astype(BF16)

    def stage_c(k):
        return remote(cgs, cg.at[own_rows], c_ss.at[k], c_rs.at[k], at_group((g + k) % groups))

    for k in range(1, groups):
        stage_c(k).start()
    cg[own_rows] = cgs[...]

    lax.fori_loop(2, 3, local, 0)

    for k in range(1, groups):
        stage_c(k).wait_recv()
    rb[...] = dot(oh[...], cg[...]).astype(BF16)

    def stage_d(k):
        return remote(
            rb.at[pl.ds(128 * k, 128)], cf.at[h, x], d_ss.at[k], d_rs.at[k],
            at_member((m + GM - k) % GM),
        )

    for k in range(1, GM):
        stage_d(k).start()
    cf[h, x] = rb[0:128]
    lax.fori_loop(3, 4, local, 0)
    for k in range(1, GM):
        stage_d(k).wait_recv()

    for w in range(2):
        for e in range(2):
            both = cf[0, 2 * w + e] + cf[1, 2 * w + e]
            for p in range(4):
                for q in range(2):
                    i = 2 * w + q
                    cbig[p, 32 * i : 32 * i + 32, 256 * i + 128 * e : 256 * i + 128 * e + 128] = both[
                        32 * p : 32 * p + 32
                    ]
    for p in range(4):
        part = dot(bp[p, 448:512], cbig[p])
        yr[64 * p : 64 * p + 64] = (yor[p, 64:128] + part).astype(BF16)

    def back(b):
        return remote(
            hs2.at[pl.ds(128 * b, 128)], hr2.at[pl.ds(128 * b, 128)],
            hs2_sem.at[b], hr2_sem.at[b], lower if b == 0 else upper,
        )

    hs2[...] = dot(sel_rt[...], yr[...]).astype(BF16)
    for b in range(2):
        back(b).start()

    def coarse_own(p, carry):
        rows = pl.ds(pl.multiple_of(CORE * p, CORE), CORE)
        part = dot(bp[p, 0:448], cbig[p])
        own[rows] += part[0:CORE]
        yo[pl.ds(pl.multiple_of(64 * p, 64), 64)] = (yor[p, 0:64] + part[CORE:448]).astype(BF16)
        return carry

    lax.fori_loop(0, 4, coarse_own, 0)

    def spread(t, carry):
        rows = pl.ds(pl.multiple_of(CORE * t, CORE), CORE)
        own[rows] += dot(sel_ot[rows], yo[...])
        return carry

    lax.fori_loop(0, 4, spread, 0)

    for b in range(2):
        back(b).wait_recv()

    def finish(t, carry):
        rows = pl.ds(pl.multiple_of(CORE * t, CORE), CORE)
        block = (own[rows] + dot(sst[rows], hr2[...])).astype(BF16)
        for i in range(4):
            out_ref[i // 2, i % 2, rows] = block[:, 256 * i : 256 * i + 256]
        return carry

    lax.fori_loop(0, 4, finish, 0)

    for b in range(2):
        halo_out(b).wait_send()
        back(b).wait_send()
    for k in range(1, GM):
        cb_out(k).wait_send()
        stage_a(k).wait_send()
        stage_d(k).wait_send()
    for k in range(1, groups):
        stage_b(k).wait_send()
        stage_c(k).wait_send()

    @pl.when(x == holder)
    def _():
        for k in range(1, XS):
            ci_out(k).wait_send()


def solution(mesh):
    groups = mesh.shape["patch"] // 2
    per_owner = 32 // groups
    vm = pltpu.VMEM
    dma = pltpu.SemaphoreType.DMA
    scratch = [
        vm((NODE, 1024), BF16), vm((8, 1024, 1024), BF16), vm((4, 2, 32, 1024), BF16),
        vm((16, 2, 32, 32), BF16), vm((per_owner, 2, 32, 32), BF16),
        vm((4, 1, PN), F32),
        vm((256, NODE), BF16), vm((NODE, 256), BF16),
        vm((256, NODE), BF16), vm((NODE, 256), BF16),
        vm((256, 256), BF16), vm((256, 256), BF16),
        vm((4, PN, PN), BF16), vm((4, PN, PN), BF16),
        vm((256, 1024), BF16), vm((256, 1024), BF16),
        vm((256, 1024), BF16), vm((256, 1024), BF16),
        vm((4, PN, 1024), BF16), vm((4, 2, 1024, 256), BF16),
        vm((4, PN, 128), BF16), vm((4, 128, PN), BF16), vm((4, 128, 1024), BF16),
        vm((NODE, 1024), F32), vm((4, 128, 1024), F32),
        vm((256, 1024), BF16), vm((256, 1024), BF16),
        vm((8, 128), F32), vm((GM, 8, 128), F32),
        vm((HALF, HALF), BF16), vm((HALF, HALF), BF16),
        vm((4, 128, 128), BF16), vm((HALF, 128), BF16), vm((HALF, 128), BF16),
        vm((groups, 32 * per_owner, 128), BF16), vm((32 * per_owner, 128), BF16),
        vm((HALF, 128), BF16), vm((HALF, 128), BF16), vm((2, 4, 128, 128), BF16),
        dma((6,)), dma((8,)), dma((2,)), dma((2,)), dma((2,)), dma((2,)),
        dma((GM,)), dma((GM,)), dma((XS,)), dma,
        dma((GM,)), dma((GM,)), dma((groups,)), dma((groups,)),
        dma((groups,)), dma((groups,)), dma((GM,)), dma((GM,)),
    ]

    def per_device(residual, patch_inv, coarse_basis, coarse_inv, patch_slots, send_rows, coarse_block):
        hbm = pl.BlockSpec(memory_space=pl.ANY)
        vmem = pl.BlockSpec(memory_space=pltpu.VMEM)
        return pl.pallas_call(
            functools.partial(kernel, groups),
            out_shape=jax.ShapeDtypeStruct(residual.shape, BF16),
            in_specs=[hbm, hbm, hbm, hbm, vmem, vmem, pl.BlockSpec(memory_space=pltpu.SMEM)],
            out_specs=vmem,
            scratch_shapes=scratch,
            compiler_params=pltpu.CompilerParams(
                collective_id=0, has_side_effects=True, vmem_limit_bytes=62 * 1024 * 1024
            ),
        )(residual, patch_inv, jnp.swapaxes(coarse_basis, 2, 3), coarse_inv, patch_slots, send_rows, coarse_block)

    node = P(None, None, ("patch", "coarse"), None)
    both = ("patch", "coarse")
    return jax.shard_map(
        per_device,
        mesh=mesh,
        in_specs=(
            node, P(both, None, None, None), P(both, None, None, None),
            P("coarse", None, None, None), P(both, None), P(both, None, None), P(both),
        ),
        out_specs=node,
        check_vma=False,
    )
```
